32 devices in a mesh: dp: 16 (over z, y, core), fsdp: 2 (over x).
Axes of the slice: x: 2, y: 2, z: 4, core: 2. Of those that a mesh axis runs over, the one named last changes fastest.
Arguments:
- tokens: bfloat16 [32768, 1024], P(('dp', 'fsdp')), may hold values from -6 to 6
- segment_ids: int32 [32768], P(('dp', 'fsdp')), may hold values from 0 to 32, as said below
- positions: int32 [32768], P(('dp', 'fsdp')), may hold values from 0 to 1982, as said below
- attn_gain: bfloat16 [1024], P('fsdp'), may hold values from 0.25 to 1.75
- qkv_weight: bfloat16 [1024, 3072], P('fsdp'), may hold values from -0.1875 to 0.1875
- attn_out_weight: bfloat16 [1024, 1024], P('fsdp'), may hold values from -0.75 to 0.75
- mlp_gain: bfloat16 [1024], P('fsdp'), may hold values from 0.25 to 1.75
- mlp_in_weight: bfloat16 [1024, 5248], P('fsdp'), may hold values from -0.1875 to 0.1875
- mlp_out_weight: bfloat16 [2624, 1024], P('fsdp'), may hold values from -0.125 to 0.125
- out_cotangent: bfloat16 [32768, 1024], P(('dp', 'fsdp')), may hold values from -6 to 6
Outputs:
- layer_out: bfloat16 [32768, 1024], P(('dp', 'fsdp'))
- grad_tokens: float32 [32768, 1024], P(('dp', 'fsdp'))
- grad_attn_gain: float32 [1024], P('fsdp')
- grad_qkv_weight: float32 [1024, 3072], P('fsdp')
- grad_attn_out_weight: float32 [1024, 1024], P('fsdp')
- grad_mlp_gain: float32 [1024], P('fsdp')
- grad_mlp_in_weight: float32 [1024, 5248], P('fsdp')
- grad_mlp_out_weight: float32 [2624, 1024], P('fsdp')
The draws below stay inside these ranges and needn't reach their ends.
Inputs may be any that keep to these rules, and one draw needn't show every extreme that they name: `segment_ids`: documents are numbered in stream order from 0. Each aligned block of 1024 tokens holds exactly one document start, which lies 64 or more tokens after the block's first token; the stream's first token also starts a document. `positions`: counts tokens since the first token of the token's document, following segment_ids; the longest document holds 1983 tokens.
All inputs are finite; a program needn't handle non-finite values.
Results may differ from the reference program's by a relative error of at most 0.024.
Values may be sent and summed in bfloat16 or wider, within the bound.
A program may use at most 256 MiB of HBM per device.

```python
import jax
import jax.numpy as jnp
from jax import lax

D = 1024
HEADS = 16
HEAD_DIM = 64
FF = 2624
HALF = 64
QBLOCK = 512
TOK_DEV = 1024
TOKENS = 32768


def block_starts(key):
    blocks = TOKENS // TOK_DEV
    first_key, second_key = jax.random.split(key)
    starts = jax.random.randint(first_key, (blocks,), HALF, TOK_DEV, dtype=jnp.int32)
    chosen = jax.random.randint(second_key, (), 0, blocks - 1, dtype=jnp.int32)
    block_index = jnp.arange(blocks, dtype=jnp.int32)
    starts = jnp.where(block_index == chosen, HALF, starts)
    starts = jnp.where(block_index == chosen + 1, TOK_DEV - 1, starts)
    return starts.astype(jnp.int32)


def draw_segment_ids(key, part):
    starts = block_starts(key)
    blocks = TOKENS // TOK_DEV
    local_index = jnp.arange(TOK_DEV, dtype=jnp.int32)
    owner = jnp.arange(blocks, dtype=jnp.int32)
    labels = owner[:, None] + (local_index[None, :] >= starts[:, None]).astype(jnp.int32)
    return labels.reshape(-1)


def draw_positions(key, part):
    starts = block_starts(key)
    blocks = TOKENS // TOK_DEV
    local_index = jnp.arange(TOK_DEV, dtype=jnp.int32)
    owner = jnp.arange(blocks, dtype=jnp.int32)
    previous = jnp.concatenate([jnp.zeros((1,), jnp.int32), starts[:-1]])
    current_begin = owner * TOK_DEV + starts
    earlier_begin = jnp.where(owner > 0, (owner - 1) * TOK_DEV + previous, 0)
    stream_index = owner[:, None] * TOK_DEV + local_index[None, :]
    begin = jnp.where(local_index[None, :] >= starts[:, None], current_begin[:, None], earlier_begin[:, None])
    return (stream_index - begin).reshape(-1)


def shard_levels(rng, dims, cuts, low, largest):
    level = 1.0
    for position, shards_of in cuts:
        heights = jax.random.uniform(jax.random.fold_in(jax.random.fold_in(rng, 6), position), (shards_of,), jnp.float32, low / len(cuts), largest / len(cuts))
        level = level * jnp.repeat(jnp.exp(heights), dims[position] // shards_of).reshape((-1,) + (1,) * (len(dims) - 1 - position))
    return level


def scatter_about(own_key, extent, scale, limit, cuts=(), held_as=jnp.bfloat16):
    entries = jax.random.normal(own_key, extent, jnp.float32) * scale
    if len(cuts) > 0:
        entries = shard_levels(own_key, extent, cuts, -0.22, 0.18) * entries
    return jnp.clip(entries, min=-limit, max=limit).astype(held_as)


def setup_inputs(seed: int = 0) -> dict:
    key_of = jax.random.split(jax.random.key(seed), 11)
    return {
        "tokens": scatter_about(key_of[0], (TOKENS, D), 1.0, 6.0, ((0, 32),)),
        "segment_ids": draw_segment_ids(jax.random.fold_in(key_of[10], 71), 0),
        "positions": draw_positions(jax.random.fold_in(key_of[10], 71), 0),
        "attn_gain": jnp.clip(1.0 + 0.15 * jax.random.normal(key_of[3], (D,), jnp.float32), 0.25, 1.75).astype(jnp.bfloat16),
        "qkv_weight": scatter_about(key_of[4], (D, 3 * D), D ** -0.5, 0.1875, ((0, 2),)),
        "attn_out_weight": scatter_about(key_of[5], (D, D), (D // 16) ** -0.5, 0.75, ((0, 2),)),
        "mlp_gain": jnp.clip(1.0 + 0.15 * jax.random.normal(key_of[6], (D,), jnp.float32), 0.25, 1.75).astype(jnp.bfloat16),
        "mlp_in_weight": scatter_about(key_of[7], (D, 2 * FF), D ** -0.5, 0.1875, ((0, 2),)),
        "mlp_out_weight": scatter_about(key_of[8], (FF, D), FF ** -0.5, 0.125, ((0, 2),)),
        "out_cotangent": scatter_about(key_of[9], (TOKENS, D), 1.0, 6.0, ((0, 32),)),
    }


@jax.custom_vjp
def low(v):
    return lax.optimization_barrier(v.astype(jnp.bfloat16)).astype(jnp.float32)

@jax.custom_vjp
def low_back(v):
    return v

def low_keep(v):
    return (low(v), None)

def low_pass(kept, grad):
    return (grad,)

def back_keep(v):
    return (v, None)

def back_low(kept, grad):
    return (low(grad),)
low.defvjp(low_keep, low_pass)
low_back.defvjp(back_keep, back_low)
HIGHEST = lax.Precision.HIGHEST
EPSILON = 1e-05
MASKED = -1e+30

def layer_norm(values, gain):
    average = lax.optimization_barrier(jnp.mean(values, axis=-1, keepdims=True))
    centred = values - average
    spread = lax.optimization_barrier(jnp.mean(centred * centred, axis=-1, keepdims=True))
    return centred * lax.rsqrt(spread + EPSILON) * gain

def rotate(values, angles):
    half_dim = values.shape[-1] // 2
    cosine_table = jnp.cos(angles)[:, None, :]
    sine_table = jnp.sin(angles)[:, None, :]
    first_half = values[..., :half_dim]
    second_half = values[..., half_dim:]
    return jnp.concatenate([first_half * cosine_table - second_half * sine_table, second_half * cosine_table + first_half * sine_table], axis=-1)

def reference(tokens, segment_ids, positions, attn_gain, qkv_weight, attn_out_weight, mlp_gain, mlp_in_weight, mlp_out_weight, out_cotangent):
    frequency = jnp.power(10000.0, -jnp.arange(0, HEAD_DIM, 2, dtype=jnp.float32) / HEAD_DIM)
    angles = positions.astype(jnp.float32)[:, None] * frequency[None, :]
    score_scale = 1.0 / HEAD_DIM ** 0.5
    seg_padded = jnp.pad(segment_ids, (HALF, HALF), constant_values=-1)
    key_span = QBLOCK + 2 * HALF

    def forward(inputs_f, gain_one, w_qkv, w_attn, gain_two, w_in, w_out):
        rows_all = inputs_f.shape[0]
        normed = low(layer_norm(inputs_f, gain_one))
        qkv = low_back(jnp.dot(normed, w_qkv, precision=HIGHEST))
        query = low(rotate(qkv[:, :D].reshape(rows_all, HEADS, HEAD_DIM), angles))
        keys = low(rotate(qkv[:, D:2 * D].reshape(rows_all, HEADS, HEAD_DIM), angles))
        values = low(qkv[:, 2 * D:].reshape(rows_all, HEADS, HEAD_DIM))
        padding = ((HALF, HALF), (0, 0), (0, 0))
        keys_pad = jnp.pad(keys, padding)
        values_pad = jnp.pad(values, padding)

        def attend(first_row):
            query_block = lax.dynamic_slice_in_dim(query, first_row, QBLOCK, 0)
            key_block = lax.dynamic_slice_in_dim(keys_pad, first_row, key_span, 0)
            value_block = lax.dynamic_slice_in_dim(values_pad, first_row, key_span, 0)
            seg_query = lax.dynamic_slice_in_dim(segment_ids, first_row, QBLOCK, 0)
            seg_key = lax.dynamic_slice_in_dim(seg_padded, first_row, key_span, 0)
            query_index = jnp.arange(QBLOCK, dtype=jnp.int32)[:, None]
            key_index = jnp.arange(key_span, dtype=jnp.int32)[None, :] - HALF
            visible = (jnp.abs(query_index - key_index) <= HALF) & (seg_query[:, None] == seg_key[None, :])
            scores = low_back(jnp.einsum('qhd,khd->hqk', query_block, key_block, precision=HIGHEST) * score_scale)
            scores = jnp.where(visible[None], scores, MASKED)
            highest = lax.optimization_barrier(jnp.max(scores, axis=-1, keepdims=True))
            expo_scores = jnp.exp(scores - highest)
            probs = low(expo_scores / lax.optimization_barrier(jnp.sum(expo_scores, axis=-1, keepdims=True)))
            mixed_heads = jnp.einsum('hqk,khd->qhd', probs, value_block, precision=HIGHEST)
            return mixed_heads.reshape(QBLOCK, D)
        block_rows = jnp.arange(rows_all // QBLOCK, dtype=jnp.int32) * QBLOCK
        attended = lax.map(jax.checkpoint(attend), block_rows).reshape(rows_all, D)
        attended = low(low_back(attended))
        resid = inputs_f + low_back(jnp.dot(attended, w_attn, precision=HIGHEST))

        def feed_forward(resid_rows):
            normed_two = low(layer_norm(resid_rows, gain_two))
            projected = low_back(jnp.dot(normed_two, w_in, precision=HIGHEST))
            activated = jax.nn.gelu(projected[:, :FF], approximate=False)
            product = low(activated * projected[:, FF:])
            return resid_rows + jnp.dot(product, w_out, precision=HIGHEST)
        result = lax.map(jax.checkpoint(feed_forward), resid.reshape(-1, TOK_DEV, D))
        return result.reshape(rows_all, D)
    primals = (tokens.astype(jnp.float32), attn_gain.astype(jnp.float32), qkv_weight.astype(jnp.float32), attn_out_weight.astype(jnp.float32), mlp_gain.astype(jnp.float32), mlp_in_weight.astype(jnp.float32), mlp_out_weight.astype(jnp.float32))
    output, pullback = jax.vjp(forward, *primals)
    gradients = pullback(out_cotangent.astype(jnp.float32))
    return (output.astype(jnp.bfloat16), gradients[0], gradients[1], gradients[2], gradients[3], gradients[4], gradients[5], gradients[6])
```

```python
import jax
import jax.numpy as jnp
from jax import lax
from jax.experimental import pallas as pl
from jax.experimental.pallas import tpu as pltpu
from jax.sharding import PartitionSpec as P

HEADS = 16
HALF = 64
QROWS = 128
KSPAN = QROWS + 2 * HALF
LANES = 128

EPSILON = 1e-05
MASKED = -1e30
STREAM = ("dp", "fsdp")
NT = (((1,), (1,)), ((), ()))
TN = (((0,), (0,)), ((), ()))
F32 = jnp.float32
BF16 = jnp.bfloat16


def passed_along(x, axis, by):
    devices = lax.axis_size(axis)
    pairs = [(i, i + by) for i in range(devices) if 0 <= i + by < devices]
    return lax.ppermute(x, axis, pairs)


def norm_forward(values, gain):
    average = jnp.mean(values, axis=-1, keepdims=True)
    centred = values - average
    inverse = lax.rsqrt(jnp.mean(centred * centred, axis=-1, keepdims=True) + EPSILON)
    scaled = centred * inverse
    return (scaled * gain, scaled, inverse)


def norm_backward(incoming, gain, scaled, inverse):
    weighted = incoming * gain
    inner = weighted - jnp.mean(weighted, axis=-1, keepdims=True)
    inner = inner - scaled * jnp.mean(weighted * scaled, axis=-1, keepdims=True)
    return (inner * inverse, jnp.sum(incoming * scaled, axis=0))


def exact_gelu(values):
    return jax.nn.gelu(values, approximate=False)


def params(limit=48):
    return pltpu.CompilerParams(vmem_limit_bytes=limit * 1024 * 1024)


def turned(x, cosine, sine):
    lane = lax.broadcasted_iota(jnp.int32, x.shape, 1)
    swapped = jnp.where(
        lane % 64 < 32, pltpu.roll(x, LANES - 32, 1), pltpu.roll(x, 32, 1)
    )
    return x * cosine + swapped * sine


def qkv_kernel(act_ref, w_ref, cos_ref, sin_ref, out_ref):
    step = pl.program_id(0)
    width = out_ref.shape[1]
    per_part = pl.num_programs(0) // 3
    rows = act_ref.shape[0]
    chunk = 256

    def product(first):
        return jnp.dot(act_ref[first : first + chunk, :], w_ref[...], preferred_element_type=F32)

    @pl.when(step < 2 * per_part)
    def _():
        scale = jnp.where(step < per_part, 0.125, 1.0).astype(F32)
        for first in range(0, rows, chunk):
            x = product(first)
            cosine = cos_ref[first : first + chunk, :]
            sine = sin_ref[first : first + chunk, :]
            for lo in range(0, width, LANES):
                part = turned(x[:, lo : lo + LANES], cosine, sine) * scale
                out_ref[first : first + chunk, lo : lo + LANES] = part.astype(BF16)

    @pl.when(step >= 2 * per_part)
    def _():
        for first in range(0, rows, chunk):
            out_ref[first : first + chunk, :] = product(first).astype(BF16)


def project_qkv(act, w, cosine, sine):
    rows, depth = act.shape
    total = w.shape[1]
    width = 256
    return pl.pallas_call(
        qkv_kernel,
        grid=(total // width,),
        in_specs=[
            pl.BlockSpec((rows, depth), lambda j: (0, 0)),
            pl.BlockSpec((depth, width), lambda j: (0, j)),
            pl.BlockSpec((rows, LANES), lambda j: (0, 0)),
            pl.BlockSpec((rows, LANES), lambda j: (0, 0)),
        ],
        out_specs=pl.BlockSpec((rows, width), lambda j: (0, j)),
        out_shape=jax.ShapeDtypeStruct((rows, total), BF16),
        compiler_params=params(),
        cost_estimate=pl.CostEstimate(
            flops=2 * rows * depth * total, bytes_accessed=2 * (rows * depth + depth * total + rows * total), transcendentals=0
        ),
    )(act, w, cosine, sine)


def head_masks():
    first = lax.broadcasted_iota(jnp.int32, (QROWS, LANES), 1) < 64
    one = jnp.where(first, 1.0, 0.0).astype(BF16)
    two = jnp.where(first, 0.0, 1.0).astype(BF16)
    return first, one, two


def attend_kernel(q_ref, k_ref, v_ref, lk_ref, lv_ref, hk_ref, hv_ref, bias_ref, out_ref, lse_ref):
    keys = jnp.concatenate([lk_ref[...], k_ref[...], hk_ref[...]], axis=0)
    values = jnp.concatenate([lv_ref[...], v_ref[...], hv_ref[...]], axis=0)
    first, one, two = head_masks()
    for b in range(q_ref.shape[0] // QROWS):
        at = b * QROWS
        q = q_ref[at : at + QROWS, :]
        pair = jnp.concatenate([q * one, q * two], axis=0)
        bias = bias_ref[b]
        scores = lax.dot_general(keys[at : at + KSPAN], pair, NT, preferred_element_type=F32)
        scores = scores + jnp.concatenate([bias, bias], axis=1)
        highest = jnp.max(scores, axis=0, keepdims=True)
        expo = jnp.exp(scores - highest)
        totals = jnp.sum(expo, axis=0, keepdims=True)
        probs = (expo * (1.0 / totals)).astype(BF16)
        mixed = lax.dot_general(probs, values[at : at + KSPAN], TN, preferred_element_type=F32)
        out_ref[at : at + QROWS, :] = jnp.where(first, mixed[:QROWS], mixed[QROWS:]).astype(BF16)
        lse_ref[b : b + 1, :] = highest + jnp.log(totals)


def halo_specs(pairs):
    return [
        pl.BlockSpec((HALF, LANES), lambda j: (0, j)),
        pl.BlockSpec((HALF, LANES), lambda j, p=pairs: (0, p + j)),
    ]


def attention(qkv, low, high, bias):
    rows = qkv.shape[0]
    width = qkv.shape[1] // 3
    pairs = width // LANES
    blocks = rows // QROWS
    column = lambda by: pl.BlockSpec((rows, LANES), lambda j, by=by: (0, by + j))
    return pl.pallas_call(
        attend_kernel,
        grid=(pairs,),
        in_specs=[column(0), column(pairs), column(2 * pairs)]
        + halo_specs(pairs)
        + halo_specs(pairs)
        + [pl.BlockSpec((blocks, KSPAN, QROWS), lambda j: (0, 0, 0))],
        out_specs=[
            pl.BlockSpec((rows, LANES), lambda j: (0, j)),
            pl.BlockSpec((None, blocks, 2 * QROWS), lambda j: (j, 0, 0)),
        ],
        out_shape=[
            jax.ShapeDtypeStruct((rows, width), BF16),
            jax.ShapeDtypeStruct((pairs, blocks, 2 * QROWS), F32),
        ],
        compiler_params=params(),
        cost_estimate=pl.CostEstimate(
            flops=16 * rows * KSPAN * width, bytes_accessed=8 * rows * width, transcendentals=rows * KSPAN * 16
        ),
    )(qkv, qkv, qkv, low, low, high, high, bias)


def attend_back_kernel(
    q_ref, k_ref, v_ref, lk_ref, lv_ref, hk_ref, hv_ref, bias_ref, do_ref, lse_ref, cos_ref, sin_ref,
    dq_ref, dk_ref, dv_ref, dlk_ref, dlv_ref, dhk_ref, dhv_ref,
):
    keys = jnp.concatenate([lk_ref[...], k_ref[...], hk_ref[...]], axis=0)
    values = jnp.concatenate([lv_ref[...], v_ref[...], hv_ref[...]], axis=0)
    first, one, two = head_masks()
    blocks = q_ref.shape[0] // QROWS
    carry_k = carry_v = None
    for b in range(blocks):
        at = b * QROWS
        q = q_ref[at : at + QROWS, :]
        pair = jnp.concatenate([q * one, q * two], axis=0)
        do = do_ref[at : at + QROWS, :]
        do_pair = jnp.concatenate([do * one, do * two], axis=0)
        key = keys[at : at + KSPAN]
        bias = bias_ref[b]
        scores = lax.dot_general(key, pair, NT, preferred_element_type=F32)
        scores = scores + jnp.concatenate([bias, bias], axis=1)
        probs = jnp.exp(scores - lse_ref[b : b + 1, :])
        dp = lax.dot_general(values[at : at + KSPAN], do_pair, NT, preferred_element_type=F32)
        centre = jnp.sum(probs * dp, axis=0, keepdims=True)
        ds = (probs * (dp - centre)).astype(BF16)
        dk = jnp.dot(ds, pair, preferred_element_type=F32)
        dv = jnp.dot(probs.astype(BF16), do_pair, preferred_element_type=F32)
        dq = lax.dot_general(ds, key, TN, preferred_element_type=F32)
        dq = jnp.where(first, dq[:QROWS], dq[QROWS:]) * 0.125
        dq_ref[at : at + QROWS, :] = turned(
            dq, cos_ref[at : at + QROWS, :], -sin_ref[at : at + QROWS, :]
        ).astype(BF16)
        head_k, head_v = dk[:QROWS], dv[:QROWS]
        if b == 0:
            dlk_ref[...] = head_k[:HALF].astype(BF16)
            dlv_ref[...] = head_v[:HALF].astype(BF16)
            dk_ref[:HALF, :] = head_k[HALF:]
            dv_ref[:HALF, :] = head_v[HALF:]
        else:
            dk_ref[at - HALF : at + HALF, :] = carry_k + head_k
            dv_ref[at - HALF : at + HALF, :] = carry_v + head_v
        carry_k, carry_v = dk[QROWS:], dv[QROWS:]
    end = blocks * QROWS
    dk_ref[end - HALF :, :] = carry_k[:HALF]
    dv_ref[end - HALF :, :] = carry_v[:HALF]
    dhk_ref[...] = carry_k[HALF:].astype(BF16)
    dhv_ref[...] = carry_v[HALF:].astype(BF16)


def attention_back(qkv, low, high, bias, grad_out, lse, cosine, sine):
    rows = qkv.shape[0]
    width = qkv.shape[1] // 3
    pairs = width // LANES
    blocks = rows // QROWS
    column = lambda by: pl.BlockSpec((rows, LANES), lambda j, by=by: (0, by + j))
    edge = pl.BlockSpec((HALF, LANES), lambda j: (0, j))
    table = pl.BlockSpec((rows, LANES), lambda j: (0, 0))
    return pl.pallas_call(
        attend_back_kernel,
        grid=(pairs,),
        in_specs=[column(0), column(pairs), column(2 * pairs)]
        + halo_specs(pairs)
        + halo_specs(pairs)
        + [
            pl.BlockSpec((blocks, KSPAN, QROWS), lambda j: (0, 0, 0)),
            column(0),
            pl.BlockSpec((None, blocks, 2 * QROWS), lambda j: (j, 0, 0)),
            table,
            table,
        ],
        out_specs=[column(0)] * 3 + [edge] * 4,
        out_shape=[jax.ShapeDtypeStruct((rows, width), BF16)]
        + [jax.ShapeDtypeStruct((rows, width), F32)] * 2
        + [jax.ShapeDtypeStruct((HALF, width), BF16)] * 4,
        compiler_params=params(),
        cost_estimate=pl.CostEstimate(
            flops=40 * rows * KSPAN * width, bytes_accessed=20 * rows * width, transcendentals=rows * KSPAN * 16
        ),
    )(qkv, qkv, qkv, low, low, high, high, bias, grad_out, lse, cosine, sine)


def join_kernel(dq_ref, dk_ref, dv_ref, lo_ref, hi_ref, cos_ref, sin_ref, out_ref):
    step = pl.program_id(0)
    per_part = pl.num_programs(0) // 3
    rows = out_ref.shape[0]

    def with_edges(ref):
        return jnp.concatenate(
            [
                ref[:HALF, :] + lo_ref[...].astype(F32),
                ref[HALF : rows - HALF, :],
                ref[rows - HALF :, :] + hi_ref[...].astype(F32),
            ],
            axis=0,
        )

    @pl.when(step < per_part)
    def _():
        out_ref[...] = dq_ref[...]

    @pl.when((step >= per_part) & (step < 2 * per_part))
    def _():
        out_ref[...] = turned(with_edges(dk_ref), cos_ref[...], -sin_ref[...]).astype(BF16)

    @pl.when(step >= 2 * per_part)
    def _():
        out_ref[...] = with_edges(dv_ref).astype(BF16)


def join_grads(dq, dk, dv, from_below, from_above, cosine, sine):
    rows, width = dq.shape
    pairs = width // LANES
    part = lambda by: pl.BlockSpec(
        (rows, LANES), lambda j, by=by: (0, jnp.clip(j - by, 0, pairs - 1))
    )
    edge = pl.BlockSpec((HALF, LANES), lambda j: (0, jnp.maximum(j - pairs, 0)))
    table = pl.BlockSpec((rows, LANES), lambda j: (0, 0))
    return pl.pallas_call(
        join_kernel,
        grid=(3 * pairs,),
        in_specs=[part(0), part(pairs), part(2 * pairs), edge, edge, table, table],
        out_specs=pl.BlockSpec((rows, LANES), lambda j: (0, j)),
        out_shape=jax.ShapeDtypeStruct((rows, 3 * width), BF16),
        compiler_params=params(),
        cost_estimate=pl.CostEstimate(flops=8 * rows * width, bytes_accessed=16 * rows * width, transcendentals=0),
    )(dq, dk, dv, from_below, from_above, cosine, sine)


def visible_bias(segment_ids, positions):
    rows = segment_ids.shape[0]
    blocks = rows // QROWS
    rank = lax.axis_index(STREAM)
    stream_len = rows * lax.axis_size(STREAM)
    edge = jnp.full((HALF,), -1, jnp.int32)
    seg_padded = jnp.concatenate([edge, segment_ids, edge])
    seg_key = jnp.stack([seg_padded[b * QROWS : b * QROWS + KSPAN] for b in range(blocks)])
    seg_key = seg_key[:, :, None]
    seg_query = segment_ids.reshape(blocks, 1, QROWS)
    pos_query = positions.reshape(blocks, 1, QROWS)
    shape = (blocks, KSPAN, QROWS)
    base = lax.broadcasted_iota(jnp.int32, shape, 0) * QROWS
    query_index = base + lax.broadcasted_iota(jnp.int32, shape, 2)
    key_index = base + lax.broadcasted_iota(jnp.int32, shape, 1) - HALF
    nearby = jnp.abs(query_index - key_index) <= HALF
    global_key = rank * rows + key_index
    inside = (global_key >= 0) & (global_key < stream_len)
    earlier_doc = pos_query >= query_index - key_index
    later_doc = seg_query == segment_ids[rows - 1]
    joined = jnp.where(
        key_index < 0, earlier_doc, jnp.where(key_index >= rows, later_doc, seg_query == seg_key)
    )
    return jnp.where(nearby & inside & joined, 0.0, MASKED).astype(F32)


def quads():
    depth, wide = lax.axis_size("dp"), lax.axis_size("fsdp")
    return [
        [(2 * m + c) * wide + f for f in range(wide) for c in range(2)] for m in range(depth // 2)
    ]


def chips():
    return [[2 * m, 2 * m + 1] for m in range(lax.axis_size("dp") // 2)]


def same_core():
    return [[2 * m + c for m in range(lax.axis_size("dp") // 2)] for c in range(2)]


def gathered(shard):
    half = shard.shape[0] // 2
    mine = lax.dynamic_slice_in_dim(shard, (lax.axis_index("dp") % 2) * half, half, 0)
    return lax.all_gather(mine, STREAM, axis=0, tiled=True, axis_index_groups=quads())


def summed(grad):
    part = lax.psum_scatter(
        grad, STREAM, scatter_dimension=0, tiled=True, axis_index_groups=quads()
    )
    part = lax.psum(part, "dp", axis_index_groups=same_core())
    whole = lax.all_gather(part, "dp", axis=0, tiled=True, axis_index_groups=chips())
    return whole.astype(F32)


def body(
    tokens,
    segment_ids,
    positions,
    attn_gain,
    qkv_weight,
    attn_out_weight,
    mlp_gain,
    mlp_in_weight,
    mlp_out_weight,
    out_cotangent,
):
    w_qkv = gathered(qkv_weight)
    gain_one = lax.all_gather(attn_gain, "fsdp", axis=0, tiled=True)
    gain_two = lax.all_gather(mlp_gain, "fsdp", axis=0, tiled=True)
    w_attn = gathered(attn_out_weight)
    w_in = gathered(mlp_in_weight)
    w_out = gathered(mlp_out_weight)
    model_width = tokens.shape[1]
    head_dim = model_width // HEADS
    hidden = w_in.shape[1] // 2

    inputs_f = tokens.astype(F32)
    gain_one = gain_one.astype(F32)
    gain_two = gain_two.astype(F32)
    normed_one, scaled_one, inverse_one = norm_forward(inputs_f, gain_one)
    act_one = normed_one.astype(BF16)
    frequency = jnp.power(10000.0, -jnp.arange(0, head_dim, 2, dtype=F32) / head_dim)
    angles = positions.astype(F32)[:, None] * frequency[None, :]
    cosine = jnp.cos(angles)
    sine = jnp.sin(angles)
    cosine = jnp.concatenate([cosine, cosine, cosine, cosine], axis=1)
    sine = jnp.concatenate([-sine, sine, -sine, sine], axis=1)
    bias = visible_bias(segment_ids, positions)

    qkv = project_qkv(act_one, w_qkv, cosine, sine)
    low = passed_along(qkv[-HALF:, model_width:], STREAM, 1)
    high = passed_along(qkv[:HALF, model_width:], STREAM, -1)
    attended, lse = attention(qkv, low, high, bias)

    resid = inputs_f + jnp.dot(attended, w_attn, preferred_element_type=F32)
    normed_two, scaled_two, inverse_two = norm_forward(resid, gain_two)
    act_two = normed_two.astype(BF16)
    projected = jnp.dot(act_two, w_in, preferred_element_type=F32)
    gating = projected[:, hidden:]
    activated, gelu_pullback = jax.vjp(exact_gelu, projected[:, :hidden])
    product = (activated * gating).astype(BF16)
    grad_wout = jnp.einsum("nf,nd->fd", product, out_cotangent, preferred_element_type=F32)
    grad_wout = grad_wout.astype(BF16)
    layer_out = (resid + jnp.dot(product, w_out, preferred_element_type=F32)).astype(BF16)
    grad_product = jnp.einsum("nd,fd->nf", out_cotangent, w_out, preferred_element_type=F32)
    grad_upper = gelu_pullback(grad_product * gating)[0]
    grad_proj = jnp.concatenate([grad_upper, grad_product * activated], axis=1).astype(BF16)
    grad_win = jnp.einsum("nd,nf->df", act_two, grad_proj, preferred_element_type=F32)
    grad_win = grad_win.astype(BF16)
    grad_proj, grad_win, grad_wout = lax.optimization_barrier((grad_proj, grad_win, grad_wout))
    grad_act_two = jnp.einsum("nf,df->nd", grad_proj, w_in, preferred_element_type=F32)
    grad_norm_two, grad_gain_two = norm_backward(grad_act_two, gain_two, scaled_two, inverse_two)
    grad_resid = out_cotangent.astype(F32) + grad_norm_two
    grad_mixed = grad_resid.astype(BF16)
    grad_attended = jnp.einsum("ne,de->nd", grad_mixed, w_attn, preferred_element_type=F32)
    grad_attended = grad_attended.astype(BF16)
    grad_wattn = jnp.einsum("nd,ne->de", attended, grad_mixed, preferred_element_type=F32)
    grad_wattn = grad_wattn.astype(BF16)

    dq, dk, dv, dlk, dlv, dhk, dhv = attention_back(
        qkv, low, high, bias, grad_attended, lse, cosine, sine
    )
    from_above = passed_along(jnp.concatenate([dlk, dlv], axis=1), STREAM, -1)
    from_below = passed_along(jnp.concatenate([dhk, dhv], axis=1), STREAM, 1)
    grad_qkv = join_grads(dq, dk, dv, from_below, from_above, cosine, sine)
    grad_wqkv = jnp.einsum("nd,nf->df", act_one, grad_qkv, preferred_element_type=F32)
    grad_wqkv = grad_wqkv.astype(BF16)
    grad_act_one = jnp.einsum("nf,df->nd", grad_qkv, w_qkv, preferred_element_type=F32)
    grad_norm_one, grad_gain_one = norm_backward(grad_act_one, gain_one, scaled_one, inverse_one)
    grad_tokens = grad_resid + grad_norm_one
    gains = jnp.stack([grad_gain_one, grad_gain_two])
    gains = lax.psum(gains, "dp")
    gains = lax.psum_scatter(gains, "fsdp", scatter_dimension=1, tiled=True)
    return (
        layer_out,
        grad_tokens,
        gains[0],
        summed(grad_wqkv),
        summed(grad_wattn),
        gains[1],
        summed(grad_win),
        summed(grad_wout),
    )


def solution(mesh):
    placed = (
        P(("dp", "fsdp"), None),
        P(("dp", "fsdp")),
        P(("dp", "fsdp")),
        P("fsdp"),
        P("fsdp", None),
        P("fsdp", None),
        P("fsdp"),
        P("fsdp", None),
        P("fsdp", None),
        P(("dp", "fsdp"), None),
    )
    return jax.shard_map(
        body,
        mesh=mesh,
        in_specs=placed,
        out_specs=(
            P(("dp", "fsdp"), None),
            P(("dp", "fsdp"), None),
            P("fsdp"),
            P("fsdp", None),
            P("fsdp", None),
            P("fsdp"),
            P("fsdp", None),
            P("fsdp", None),
        ),
        check_vma=False,
    )
```

```python
import jax
import jax.numpy as jnp
from jax import lax
from jax.experimental import pallas as pl
from jax.experimental.pallas import tpu as pltpu
from jax.sharding import PartitionSpec as P

HEADS = 16
HALF = 64
QROWS = 128
KSPAN = QROWS + 2 * HALF
LANES = 128

EPSILON = 1e-05
MASKED = -1e30
STREAM = ("dp", "fsdp")
NT = (((1,), (1,)), ((), ()))
TN = (((0,), (0,)), ((), ()))
F32 = jnp.float32
BF16 = jnp.bfloat16


def passed_along(x, axis, by):
    devices = lax.axis_size(axis)
    pairs = [(i, i + by) for i in range(devices) if 0 <= i + by < devices]
    return lax.ppermute(x, axis, pairs)


def norm_forward(values, gain):
    average = jnp.mean(values, axis=-1, keepdims=True)
    centred = values - average
    inverse = lax.rsqrt(jnp.mean(centred * centred, axis=-1, keepdims=True) + EPSILON)
    scaled = centred * inverse
    return (scaled * gain, scaled, inverse)


def norm_backward(incoming, gain, scaled, inverse):
    weighted = incoming * gain
    inner = weighted - jnp.mean(weighted, axis=-1, keepdims=True)
    inner = inner - scaled * jnp.mean(weighted * scaled, axis=-1, keepdims=True)
    return (inner * inverse, jnp.sum(incoming * scaled, axis=0))


def exact_gelu(values):
    return jax.nn.gelu(values, approximate=False)


def params(limit=48):
    return pltpu.CompilerParams(vmem_limit_bytes=limit * 1024 * 1024)


def turned(x, cosine, sine):
    lane = lax.broadcasted_iota(jnp.int32, x.shape, 1)
    swapped = jnp.where(
        lane % 64 < 32, pltpu.roll(x, LANES - 32, 1), pltpu.roll(x, 32, 1)
    )
    return x * cosine + swapped * sine


def qkv_kernel(act_ref, w_ref, cos_ref, sin_ref, out_ref):
    step = pl.program_id(0)
    width = out_ref.shape[1]
    per_part = pl.num_programs(0) // 3
    rows = act_ref.shape[0]
    chunk = 256

    def product(first):
        return jnp.dot(act_ref[first : first + chunk, :], w_ref[...], preferred_element_type=F32)

    @pl.when(step < 2 * per_part)
    def _():
        scale = jnp.where(step < per_part, 0.125, 1.0).astype(F32)
        for first in range(0, rows, chunk):
            x = product(first)
            cosine = cos_ref[first : first + chunk, :]
            sine = sin_ref[first : first + chunk, :]
            for lo in range(0, width, LANES):
                part = turned(x[:, lo : lo + LANES], cosine, sine) * scale
                out_ref[first : first + chunk, lo : lo + LANES] = part.astype(BF16)

    @pl.when(step >= 2 * per_part)
    def _():
        for first in range(0, rows, chunk):
            out_ref[first : first + chunk, :] = product(first).astype(BF16)


def project_qkv(act, w, cosine, sine):
    rows, depth = act.shape
    total = w.shape[1]
    width = 256
    return pl.pallas_call(
        qkv_kernel,
        grid=(total // width,),
        in_specs=[
            pl.BlockSpec((rows, depth), lambda j: (0, 0)),
            pl.BlockSpec((depth, width), lambda j: (0, j)),
            pl.BlockSpec((rows, LANES), lambda j: (0, 0)),
            pl.BlockSpec((rows, LANES), lambda j: (0, 0)),
        ],
        out_specs=pl.BlockSpec((rows, width), lambda j: (0, j)),
        out_shape=jax.ShapeDtypeStruct((rows, total), BF16),
        compiler_params=params(),
        cost_estimate=pl.CostEstimate(
            flops=2 * rows * depth * total, bytes_accessed=2 * (rows * depth + depth * total + rows * total), transcendentals=0
        ),
    )(act, w, cosine, sine)


def head_masks():
    first = lax.broadcasted_iota(jnp.int32, (QROWS, LANES), 1) < 64
    one = jnp.where(first, 1.0, 0.0).astype(BF16)
    two = jnp.where(first, 0.0, 1.0).astype(BF16)
    return first, one, two


def attend_kernel(q_ref, k_ref, v_ref, lk_ref, lv_ref, hk_ref, hv_ref, bias_ref, out_ref, lse_ref):
    keys = jnp.concatenate([lk_ref[...], k_ref[...], hk_ref[...]], axis=0)
    values = jnp.concatenate([lv_ref[...], v_ref[...], hv_ref[...]], axis=0)
    first, one, two = head_masks()
    for b in range(q_ref.shape[0] // QROWS):
        at = b * QROWS
        q = q_ref[at : at + QROWS, :]
        pair = jnp.concatenate([q * one, q * two], axis=0)
        bias = bias_ref[b]
        scores = lax.dot_general(keys[at : at + KSPAN], pair, NT, preferred_element_type=F32)
        scores = scores + jnp.concatenate([bias, bias], axis=1)
        highest = jnp.max(scores, axis=0, keepdims=True)
        expo = jnp.exp(scores - highest)
        totals = jnp.sum(expo, axis=0, keepdims=True)
        probs = (expo * (1.0 / totals)).astype(BF16)
        mixed = lax.dot_general(probs, values[at : at + KSPAN], TN, preferred_element_type=F32)
        out_ref[at : at + QROWS, :] = jnp.where(first, mixed[:QROWS], mixed[QROWS:]).astype(BF16)
        lse_ref[b : b + 1, :] = highest + jnp.log(totals)


def halo_specs(pairs):
    return [
        pl.BlockSpec((HALF, LANES), lambda j: (0, j)),
        pl.BlockSpec((HALF, LANES), lambda j, p=pairs: (0, p + j)),
    ]


def attention(qkv, low, high, bias):
    rows = qkv.shape[0]
    width = qkv.shape[1] // 3
    pairs = width // LANES
    blocks = rows // QROWS
    column = lambda by: pl.BlockSpec((rows, LANES), lambda j, by=by: (0, by + j))
    return pl.pallas_call(
        attend_kernel,
        grid=(pairs,),
        in_specs=[column(0), column(pairs), column(2 * pairs)]
        + halo_specs(pairs)
        + halo_specs(pairs)
        + [pl.BlockSpec((blocks, KSPAN, QROWS), lambda j: (0, 0, 0))],
        out_specs=[
            pl.BlockSpec((rows, LANES), lambda j: (0, j)),
            pl.BlockSpec((None, blocks, 2 * QROWS), lambda j: (j, 0, 0)),
        ],
        out_shape=[
            jax.ShapeDtypeStruct((rows, width), BF16),
            jax.ShapeDtypeStruct((pairs, blocks, 2 * QROWS), F32),
        ],
        compiler_params=params(),
        cost_estimate=pl.CostEstimate(
            flops=16 * rows * KSPAN * width, bytes_accessed=8 * rows * width, transcendentals=rows * KSPAN * 16
        ),
    )(qkv, qkv, qkv, low, low, high, high, bias)


def attend_back_kernel(
    q_ref, k_ref, v_ref, lk_ref, lv_ref, hk_ref, hv_ref, bias_ref, do_ref, lse_ref, cos_ref, sin_ref,
    dq_ref, dk_ref, dv_ref, dlk_ref, dlv_ref, dhk_ref, dhv_ref,
):
    keys = jnp.concatenate([lk_ref[...], k_ref[...], hk_ref[...]], axis=0)
    values = jnp.concatenate([lv_ref[...], v_ref[...], hv_ref[...]], axis=0)
    first, one, two = head_masks()
    blocks = q_ref.shape[0] // QROWS
    carry_k = carry_v = None
    for b in range(blocks):
        at = b * QROWS
        q = q_ref[at : at + QROWS, :]
        pair = jnp.concatenate([q * one, q * two], axis=0)
        do = do_ref[at : at + QROWS, :]
        do_pair = jnp.concatenate([do * one, do * two], axis=0)
        key = keys[at : at + KSPAN]
        bias = bias_ref[b]
        scores = lax.dot_general(key, pair, NT, preferred_element_type=F32)
        scores = scores + jnp.concatenate([bias, bias], axis=1)
        probs = jnp.exp(scores - lse_ref[b : b + 1, :])
        dp = lax.dot_general(values[at : at + KSPAN], do_pair, NT, preferred_element_type=F32)
        centre = jnp.sum(probs * dp, axis=0, keepdims=True)
        ds = (probs * (dp - centre)).astype(BF16)
        dk = jnp.dot(ds, pair, preferred_element_type=F32)
        dv = jnp.dot(probs.astype(BF16), do_pair, preferred_element_type=F32)
        dq = lax.dot_general(ds, key, TN, preferred_element_type=F32)
        dq = jnp.where(first, dq[:QROWS], dq[QROWS:]) * 0.125
        dq_ref[at : at + QROWS, :] = turned(
            dq, cos_ref[at : at + QROWS, :], -sin_ref[at : at + QROWS, :]
        ).astype(BF16)
        head_k, head_v = dk[:QROWS], dv[:QROWS]
        if b == 0:
            dlk_ref[...] = head_k[:HALF].astype(BF16)
            dlv_ref[...] = head_v[:HALF].astype(BF16)
            dk_ref[:HALF, :] = head_k[HALF:]
            dv_ref[:HALF, :] = head_v[HALF:]
        else:
            dk_ref[at - HALF : at + HALF, :] = carry_k + head_k
            dv_ref[at - HALF : at + HALF, :] = carry_v + head_v
        carry_k, carry_v = dk[QROWS:], dv[QROWS:]
    end = blocks * QROWS
    dk_ref[end - HALF :, :] = carry_k[:HALF]
    dv_ref[end - HALF :, :] = carry_v[:HALF]
    dhk_ref[...] = carry_k[HALF:].astype(BF16)
    dhv_ref[...] = carry_v[HALF:].astype(BF16)


def attention_back(qkv, low, high, bias, grad_out, lse, cosine, sine):
    rows = qkv.shape[0]
    width = qkv.shape[1] // 3
    pairs = width // LANES
    blocks = rows // QROWS
    column = lambda by: pl.BlockSpec((rows, LANES), lambda j, by=by: (0, by + j))
    edge = pl.BlockSpec((HALF, LANES), lambda j: (0, j))
    table = pl.BlockSpec((rows, LANES), lambda j: (0, 0))
    return pl.pallas_call(
        attend_back_kernel,
        grid=(pairs,),
        in_specs=[column(0), column(pairs), column(2 * pairs)]
        + halo_specs(pairs)
        + halo_specs(pairs)
        + [
            pl.BlockSpec((blocks, KSPAN, QROWS), lambda j: (0, 0, 0)),
            column(0),
            pl.BlockSpec((None, blocks, 2 * QROWS), lambda j: (j, 0, 0)),
            table,
            table,
        ],
        out_specs=[column(0)] * 3 + [edge] * 4,
        out_shape=[jax.ShapeDtypeStruct((rows, width), BF16)]
        + [jax.ShapeDtypeStruct((rows, width), F32)] * 2
        + [jax.ShapeDtypeStruct((HALF, width), BF16)] * 4,
        compiler_params=params(),
        cost_estimate=pl.CostEstimate(
            flops=40 * rows * KSPAN * width, bytes_accessed=20 * rows * width, transcendentals=rows * KSPAN * 16
        ),
    )(qkv, qkv, qkv, low, low, high, high, bias, grad_out, lse, cosine, sine)


def join_kernel(dq_ref, dk_ref, dv_ref, lo_ref, hi_ref, cos_ref, sin_ref, out_ref):
    step = pl.program_id(0)
    per_part = pl.num_programs(0) // 3
    rows = out_ref.shape[0]

    def with_edges(ref):
        return jnp.concatenate(
            [
                ref[:HALF, :] + lo_ref[...].astype(F32),
                ref[HALF : rows - HALF, :],
                ref[rows - HALF :, :] + hi_ref[...].astype(F32),
            ],
            axis=0,
        )

    @pl.when(step < per_part)
    def _():
        out_ref[...] = dq_ref[...]

    @pl.when((step >= per_part) & (step < 2 * per_part))
    def _():
        out_ref[...] = turned(with_edges(dk_ref), cos_ref[...], -sin_ref[...]).astype(BF16)

    @pl.when(step >= 2 * per_part)
    def _():
        out_ref[...] = with_edges(dv_ref).astype(BF16)


def join_grads(dq, dk, dv, from_below, from_above, cosine, sine):
    rows, width = dq.shape
    pairs = width // LANES
    part = lambda by: pl.BlockSpec(
        (rows, LANES), lambda j, by=by: (0, jnp.clip(j - by, 0, pairs - 1))
    )
    edge = pl.BlockSpec((HALF, LANES), lambda j: (0, jnp.maximum(j - pairs, 0)))
    table = pl.BlockSpec((rows, LANES), lambda j: (0, 0))
    return pl.pallas_call(
        join_kernel,
        grid=(3 * pairs,),
        in_specs=[part(0), part(pairs), part(2 * pairs), edge, edge, table, table],
        out_specs=pl.BlockSpec((rows, LANES), lambda j: (0, j)),
        out_shape=jax.ShapeDtypeStruct((rows, 3 * width), BF16),
        compiler_params=params(),
        cost_estimate=pl.CostEstimate(flops=8 * rows * width, bytes_accessed=16 * rows * width, transcendentals=0),
    )(dq, dk, dv, from_below, from_above, cosine, sine)


def visible_bias(segment_ids, positions):
    rows = segment_ids.shape[0]
    blocks = rows // QROWS
    rank = lax.axis_index(STREAM)
    stream_len = rows * lax.axis_size(STREAM)
    edge = jnp.full((HALF,), -1, jnp.int32)
    seg_padded = jnp.concatenate([edge, segment_ids, edge])
    seg_key = jnp.stack([seg_padded[b * QROWS : b * QROWS + KSPAN] for b in range(blocks)])
    seg_key = seg_key[:, :, None]
    seg_query = segment_ids.reshape(blocks, 1, QROWS)
    pos_query = positions.reshape(blocks, 1, QROWS)
    shape = (blocks, KSPAN, QROWS)
    base = lax.broadcasted_iota(jnp.int32, shape, 0) * QROWS
    query_index = base + lax.broadcasted_iota(jnp.int32, shape, 2)
    key_index = base + lax.broadcasted_iota(jnp.int32, shape, 1) - HALF
    nearby = jnp.abs(query_index - key_index) <= HALF
    global_key = rank * rows + key_index
    inside = (global_key >= 0) & (global_key < stream_len)
    earlier_doc = pos_query >= query_index - key_index
    later_doc = seg_query == segment_ids[rows - 1]
    joined = jnp.where(
        key_index < 0, earlier_doc, jnp.where(key_index >= rows, later_doc, seg_query == seg_key)
    )
    return jnp.where(nearby & inside & joined, 0.0, MASKED).astype(F32)


def quads():
    depth, wide = lax.axis_size("dp"), lax.axis_size("fsdp")
    return [
        [(2 * m + c) * wide + f for f in range(wide) for c in range(2)] for m in range(depth // 2)
    ]


def gathered(shard):
    half = shard.shape[0] // 2
    mine = lax.dynamic_slice_in_dim(shard, (lax.axis_index("dp") % 2) * half, half, 0)
    return lax.all_gather(mine, STREAM, axis=0, tiled=True, axis_index_groups=quads())


def partners(axis, bit):
    return [(i, i ^ (1 << bit)) for i in range(lax.axis_size(axis))]


def halves(x, dim, axis, bit):
    side = (lax.axis_index(axis) >> bit) % 2
    size = x.shape[dim] // 2
    keep = lax.dynamic_slice_in_dim(x, side * size, size, dim)
    send = lax.dynamic_slice_in_dim(x, (1 - side) * size, size, dim)
    return keep, send


def halved(x, dim, axis, bit):
    keep, send = halves(x, dim, axis, bit)
    got = lax.ppermute(send, axis, partners(axis, bit))
    return (keep.astype(F32) + got.astype(F32)).astype(BF16)


def doubled(x, dim, axis, bit):
    got = lax.ppermute(x, axis, partners(axis, bit))
    side = (lax.axis_index(axis) >> bit) % 2
    low = jnp.where(side == 0, x, got)
    high = jnp.where(side == 0, got, x)
    return jnp.concatenate([low, high], axis=dim)


def over_cores(grad):
    wide = lax.axis_size("fsdp")
    rows, columns = grad.shape
    return halved(grad.reshape(wide, rows // wide, columns), 1, "dp", 0)


def over_fsdp(part):
    if lax.axis_size("fsdp") == 2:
        return halved(part, 0, "fsdp", 0)[0]
    return lax.psum_scatter(part, "fsdp", scatter_dimension=0, tiled=True)[0]


def over_rest(part, dim):
    levels = lax.axis_size("dp").bit_length() - 1
    for bit in range(1, levels):
        part = halved(part, dim, "dp", bit)
    for bit in reversed(range(1, levels)):
        part = doubled(part, dim, "dp", bit)
    return doubled(part, 0, "dp", 0).astype(F32)


def summed_gains(gains):
    for bit in range(lax.axis_size("dp").bit_length() - 1):
        gains = gains + lax.ppermute(gains, "dp", partners("dp", bit))
    if lax.axis_size("fsdp") == 2:
        keep, send = halves(gains, 1, "fsdp", 0)
        return keep + lax.ppermute(send, "fsdp", partners("fsdp", 0))
    return lax.psum_scatter(gains, "fsdp", scatter_dimension=1, tiled=True)


def body(
    tokens,
    segment_ids,
    positions,
    attn_gain,
    qkv_weight,
    attn_out_weight,
    mlp_gain,
    mlp_in_weight,
    mlp_out_weight,
    out_cotangent,
):
    w_qkv = gathered(qkv_weight)
    gains = jnp.stack([attn_gain, mlp_gain])
    gain_one, gain_two = lax.all_gather(gains, "fsdp", axis=1, tiled=True)
    w_attn = gathered(attn_out_weight)
    w_in = gathered(mlp_in_weight)
    w_out = gathered(mlp_out_weight)
    model_width = tokens.shape[1]
    head_dim = model_width // HEADS
    hidden = w_in.shape[1] // 2

    inputs_f = tokens.astype(F32)
    gain_one = gain_one.astype(F32)
    gain_two = gain_two.astype(F32)
    normed_one, scaled_one, inverse_one = norm_forward(inputs_f, gain_one)
    act_one = normed_one.astype(BF16)
    frequency = jnp.power(10000.0, -jnp.arange(0, head_dim, 2, dtype=F32) / head_dim)
    angles = positions.astype(F32)[:, None] * frequency[None, :]
    cosine = jnp.cos(angles)
    sine = jnp.sin(angles)
    cosine = jnp.concatenate([cosine, cosine, cosine, cosine], axis=1)
    sine = jnp.concatenate([-sine, sine, -sine, sine], axis=1)
    bias = visible_bias(segment_ids, positions)

    qkv = project_qkv(act_one, w_qkv, cosine, sine)
    low = passed_along(qkv[-HALF:, model_width:], STREAM, 1)
    high = passed_along(qkv[:HALF, model_width:], STREAM, -1)
    attended, lse = attention(qkv, low, high, bias)

    resid = inputs_f + jnp.dot(attended, w_attn, preferred_element_type=F32)
    normed_two, scaled_two, inverse_two = norm_forward(resid, gain_two)
    act_two = normed_two.astype(BF16)
    projected = jnp.dot(act_two, w_in, preferred_element_type=F32)
    gating = projected[:, hidden:]
    activated, gelu_pullback = jax.vjp(exact_gelu, projected[:, :hidden])
    product = (activated * gating).astype(BF16)
    grad_wout = jnp.einsum("nf,nd->fd", product, out_cotangent, preferred_element_type=F32)
    grad_wout = grad_wout.astype(BF16)
    layer_out = (resid + jnp.dot(product, w_out, preferred_element_type=F32)).astype(BF16)
    grad_product = jnp.einsum("nd,fd->nf", out_cotangent, w_out, preferred_element_type=F32)
    grad_upper = gelu_pullback(grad_product * gating)[0]
    grad_proj = jnp.concatenate([grad_upper, grad_product * activated], axis=1).astype(BF16)
    grad_win = jnp.einsum("nd,nf->df", act_two, grad_proj, preferred_element_type=F32)
    grad_win = grad_win.astype(BF16)
    grad_proj, grad_win, grad_wout = lax.optimization_barrier((grad_proj, grad_win, grad_wout))
    grad_act_two = jnp.einsum("nf,df->nd", grad_proj, w_in, preferred_element_type=F32)
    grad_norm_two, grad_gain_two = norm_backward(grad_act_two, gain_two, scaled_two, inverse_two)
    grad_resid = out_cotangent.astype(F32) + grad_norm_two
    grad_mixed = grad_resid.astype(BF16)
    grad_attended = jnp.einsum("ne,de->nd", grad_mixed, w_attn, preferred_element_type=F32)
    grad_attended = grad_attended.astype(BF16)
    grad_wattn = jnp.einsum("nd,ne->de", attended, grad_mixed, preferred_element_type=F32)
    grad_wattn = grad_wattn.astype(BF16)

    part_win = over_cores(grad_win)
    part_wout = over_cores(grad_wout)
    grad_attended, part_win, part_wout = lax.optimization_barrier(
        (grad_attended, part_win, part_wout)
    )
    part_win = over_fsdp(part_win)
    part_wout = over_fsdp(part_wout)
    part_wattn = over_cores(grad_wattn)

    dq, dk, dv, dlk, dlv, dhk, dhv = attention_back(
        qkv, low, high, bias, grad_attended, lse, cosine, sine
    )
    from_above = passed_along(jnp.concatenate([dlk, dlv], axis=1), STREAM, -1)
    from_below = passed_along(jnp.concatenate([dhk, dhv], axis=1), STREAM, 1)
    grad_qkv = join_grads(dq, dk, dv, from_below, from_above, cosine, sine)
    grad_wqkv = jnp.einsum("nd,nf->df", act_one, grad_qkv, preferred_element_type=F32)
    grad_wqkv = grad_wqkv.astype(BF16)
    grad_wqkv, part_win, part_wout, part_wattn, grad_qkv = lax.optimization_barrier(
        (grad_wqkv, part_win, part_wout, part_wattn, grad_qkv)
    )
    part_wqkv = over_cores(grad_wqkv)
    grad_act_one = jnp.einsum("nf,df->nd", grad_qkv, w_qkv, preferred_element_type=F32)
    grad_norm_one, grad_gain_one = norm_backward(grad_act_one, gain_one, scaled_one, inverse_one)
    grad_tokens = grad_resid + grad_norm_one
    gains = summed_gains(jnp.stack([grad_gain_one, grad_gain_two]))
    return (
        layer_out,
        grad_tokens,
        gains[0],
        over_rest(over_fsdp(part_wqkv), 0),
        over_rest(over_fsdp(part_wattn), 0),
        gains[1],
        over_rest(part_win, 0),
        over_rest(part_wout, 1),
    )


def solution(mesh):
    placed = (
        P(("dp", "fsdp"), None),
        P(("dp", "fsdp")),
        P(("dp", "fsdp")),
        P("fsdp"),
        P("fsdp", None),
        P("fsdp", None),
        P("fsdp"),
        P("fsdp", None),
        P("fsdp", None),
        P(("dp", "fsdp"), None),
    )
    return jax.shard_map(
        body,
        mesh=mesh,
        in_specs=placed,
        out_specs=(
            P(("dp", "fsdp"), None),
            P(("dp", "fsdp"), None),
            P("fsdp"),
            P("fsdp", None),
            P("fsdp", None),
            P("fsdp"),
            P("fsdp", None),
            P("fsdp", None),
        ),
        check_vma=False,
    )
```
